32 devices in a mesh: dp: 4 (over y, core), row: 2 (over x), col: 4 (over z).
Axes of the slice: x: 2, y: 2, z: 4, core: 2. Of those that a mesh axis runs over, the one named last changes fastest.
Arguments:
- tokens: bfloat16 [3072, 4096], P('dp', ('row', 'col')), may hold values from -6 to 6
- cotangent: bfloat16 [3072, 4096], P('dp', ('row', 'col')), may hold values from -4 to 4
- gate_weight: bfloat16 [4096, 14336], P('row', 'col'), may hold values from -0.09375 to 0.09375
- up_weight: bfloat16 [4096, 14336], P('row', 'col'), may hold values from -0.09375 to 0.09375
- down_weight: bfloat16 [14336, 4096], P('col', 'row'), may hold values from -0.046875 to 0.046875
Outputs:
- layer_out: bfloat16 [3072, 4096], P(('dp', 'col'), 'row')
- input_grad: bfloat16 [3072, 4096], P(('dp', 'col'), 'row')
- gate_wgrad: bfloat16 [4096, 14336], P('row', 'col')
- up_wgrad: bfloat16 [4096, 14336], P('row', 'col')
- down_wgrad: bfloat16 [14336, 4096], P('col', 'row')
The draws below stay inside these ranges and needn't reach their ends.
All inputs are finite; a program needn't handle non-finite values.
Results may differ from the reference program's by a relative error of at most 0.034.
Values may be sent and summed in bfloat16 or wider, within the bound.
A program may use at most 256 MiB of HBM per device.

```python
import jax
import jax.numpy as jnp

D = 4096
FF = 14336
TOK_GRP = 768
TOKENS = 3072
N_DP = 4
N_ROW = 2
N_COL = 4


def steps_of(own_key, shape, cuts, low, largest):
    def one(position, blocks):
        steps = jax.random.uniform(jax.random.fold_in(jax.random.fold_in(own_key, 6), position), (blocks,), jnp.float32, low / len(cuts), largest / len(cuts))
        return jnp.repeat(jnp.exp(steps), shape[position] // blocks).reshape((-1,) + (1,) * (len(shape) - position - 1))

    loudness = one(*cuts[0])
    for cut in cuts[1:]:
        loudness = loudness * one(*cut)
    return loudness


def gaussian(key, extent, spread, limit, split=(), kind=jnp.bfloat16):
    loudness = steps_of(key, extent, split, -0.22, 0.18) if split else 1.0
    entries = jax.random.normal(key, extent, jnp.float32) * spread * loudness
    return jnp.minimum(jnp.maximum(entries, -limit), limit).astype(kind)


def setup_inputs(seed: int = 0) -> dict:
    streams_of = jax.random.split(jax.random.key(seed), 6)
    tokens = gaussian(streams_of[0], (TOKENS, D), 1.0, 6.0, ((0, 4), (1, 8)))
    cotangent = gaussian(streams_of[1], (TOKENS, D), 0.25, 4.0, ((0, 4), (1, 8)))
    gate_weight = gaussian(streams_of[2], (D, FF), D ** -0.5, 0.09375, ((0, 2), (1, 4)))
    up_weight = gaussian(streams_of[3], (D, FF), D ** -0.5, 0.09375, ((0, 2), (1, 4)))
    down_weight = gaussian(streams_of[4], (FF, D), FF ** -0.5, 0.046875, ((0, 4), (1, 2)))
    return {"tokens": tokens, "cotangent": cotangent, "gate_weight": gate_weight, "up_weight": up_weight, "down_weight": down_weight}


def blocked(left, right, parts):
    width = left.shape[1] // parts
    total = jnp.zeros((left.shape[0], right.shape[1]), jnp.float32)
    for block in range(parts):
        term = jnp.dot(left[:, block * width:(block + 1) * width], right[block * width:(block + 1) * width],
                       preferred_element_type=jnp.float32)
        total = total + term.astype(jnp.bfloat16).astype(jnp.float32)
    return total


def input_blocked(gate_grad, up_grad, gate_weight, up_weight, parts):
    width = gate_grad.shape[1] // parts
    total = jnp.zeros((gate_grad.shape[0], gate_weight.shape[0]), jnp.float32)
    for block in range(parts):
        lo = block * width
        hi = lo + width
        term = (jnp.dot(gate_grad[:, lo:hi], gate_weight[:, lo:hi].T, preferred_element_type=jnp.float32)
                + jnp.dot(up_grad[:, lo:hi], up_weight[:, lo:hi].T, preferred_element_type=jnp.float32))
        total = total + term.astype(jnp.bfloat16).astype(jnp.float32)
    return total


def group_pass(x, dy, gate_weight, up_weight, down_weight):
    f32 = jnp.float32
    gate = blocked(x, gate_weight, N_ROW)
    up = blocked(x, up_weight, N_ROW)
    sigma = jax.nn.sigmoid(gate)
    silu_gate = gate * sigma
    hidden = (silu_gate * up).astype(jnp.bfloat16)
    layer_out = blocked(hidden, down_weight, N_COL).astype(jnp.bfloat16)
    hidden_grad = blocked(dy, down_weight.T, N_ROW)
    gate_grad = (hidden_grad * up * sigma * (1.0 + gate * (1.0 - sigma))).astype(jnp.bfloat16)
    up_grad = (hidden_grad * silu_gate).astype(jnp.bfloat16)
    input_grad = input_blocked(gate_grad, up_grad, gate_weight, up_weight, N_COL).astype(jnp.bfloat16)
    down_part = jnp.dot(hidden.T, dy, preferred_element_type=f32).astype(jnp.bfloat16)
    gate_part = jnp.dot(x.T, gate_grad, preferred_element_type=f32).astype(jnp.bfloat16)
    up_part = jnp.dot(x.T, up_grad, preferred_element_type=f32).astype(jnp.bfloat16)
    return layer_out, input_grad, gate_part, up_part, down_part


def reference(tokens, cotangent, gate_weight, up_weight, down_weight):
    outputs = []
    in_grads = []
    gate_total = jnp.zeros((D, FF), jnp.float32)
    up_total = jnp.zeros((D, FF), jnp.float32)
    down_total = jnp.zeros((FF, D), jnp.float32)
    for group in range(N_DP):
        x = tokens[group * TOK_GRP:(group + 1) * TOK_GRP]
        dy = cotangent[group * TOK_GRP:(group + 1) * TOK_GRP]
        layer_out, input_grad, gate_part, up_part, down_part = group_pass(x, dy, gate_weight, up_weight, down_weight)
        outputs.append(layer_out)
        in_grads.append(input_grad)
        gate_total = gate_total + gate_part.astype(jnp.float32)
        up_total = up_total + up_part.astype(jnp.float32)
        down_total = down_total + down_part.astype(jnp.float32)
    return (jnp.concatenate(outputs, axis=0), jnp.concatenate(in_grads, axis=0),
            gate_total.astype(jnp.bfloat16), up_total.astype(jnp.bfloat16), down_total.astype(jnp.bfloat16))
```

```python
import functools

import jax
import jax.numpy as jnp
from jax import lax
from jax.experimental import pallas as pl
from jax.experimental.pallas import tpu as pltpu
from jax.sharding import PartitionSpec as P

LANES = 128


def contract_rows(left, right):
    return lax.dot_general(
        left, right, (((0,), (0,)), ((), ())), preferred_element_type=jnp.float32
    )


def contract_cols(left, right):
    return lax.dot_general(
        left, right, (((1,), (1,)), ((), ())), preferred_element_type=jnp.float32
    )


def place_body(parts, outs, aliased, pos_ref, *refs):
    ins = refs[: parts * outs]
    results = refs[parts * outs + aliased :]
    step = pl.program_id(0)
    for part in range(parts):

        @pl.when(step == part)
        def _(part=part):
            for out in range(outs):
                results[out][...] = ins[part * outs + out][...]


def place(pos, pieces, previous, total, offset, width, outs, axis):
    parts = len(pieces)
    steps = width // LANES
    other = pieces[0].shape[1 - axis]
    units = parts * total

    def at(index):
        return (index, 0) if axis == 0 else (0, index)

    block = (LANES, other) if axis == 0 else (other, LANES)

    def in_spec(part, out):
        def index(j, i, pos_ref):
            own = jnp.where(j == part, i, jnp.where(j < part, 0, steps - 1))
            return at(out * steps + own)

        return pl.BlockSpec(block, index)

    def out_index(j, i, pos_ref):
        return at(pos_ref[j] * (total // LANES) + offset // LANES + i)

    shape = (units, other) if axis == 0 else (other, units)
    operands = [pieces[part] for part in range(parts) for _ in range(outs)]
    in_specs = [in_spec(part, out) for part in range(parts) for out in range(outs)]
    aliases = {}
    if previous is not None:
        for out in range(outs):
            aliases[1 + len(operands)] = out
            operands.append(previous[out])
            in_specs.append(pl.BlockSpec(memory_space=pl.ANY))
    moved = 4 * parts * outs * width * other
    return pl.pallas_call(
        functools.partial(place_body, parts, outs, 0 if previous is None else outs),
        out_shape=[jax.ShapeDtypeStruct(shape, jnp.bfloat16)] * outs,
        grid_spec=pltpu.PrefetchScalarGridSpec(
            num_scalar_prefetch=1,
            grid=(parts, steps),
            in_specs=in_specs,
            out_specs=[pl.BlockSpec(block, out_index)] * outs,
        ),
        input_output_aliases=aliases,
        compiler_params=pltpu.CompilerParams(vmem_limit_bytes=32 * 2**20),
        cost_estimate=pl.CostEstimate(flops=0, bytes_accessed=moved, transcendentals=0),
    )(pos, *operands)


def local_units(tokens, cotangent, gate_weight, up_weight, down_weight):
    f32, bf16 = jnp.float32, jnp.bfloat16
    me = lax.axis_index("dp")
    total = gate_weight.shape[1] // 4
    first = -(-total // 512) * 256
    bands = ((0, first), (first, total - first))
    rows = tokens.shape[0]

    def swap_row(a):
        return lax.ppermute(a, "row", [(0, 1), (1, 0)])

    def swap_core(a):
        return lax.ppermute(a, "dp", [(i, i ^ 1) for i in range(4)])

    def swap_y(a):
        return lax.ppermute(a, "dp", [(i, i ^ 2) for i in range(4)])

    start = me * total
    gate_w = lax.dynamic_slice_in_dim(gate_weight, start, total, 1)
    up_w = lax.dynamic_slice_in_dim(up_weight, start, total, 1)
    down_w = lax.dynamic_slice_in_dim(down_weight, start, total, 0)
    gu_w = [jnp.concatenate([gate_w[:, o : o + w], up_w[:, o : o + w]], axis=1) for o, w in bands]
    d_w = [down_w[o : o + w] for o, w in bands]

    x0 = lax.all_gather(tokens, "col", axis=1, tiled=True)
    x2 = swap_y(x0)
    x1, x3 = swap_core(x0), swap_core(x2)
    dy0 = lax.all_gather(cotangent, "col", axis=1, tiled=True)
    dy2 = swap_y(dy0)
    dy1, dy3 = swap_core(dy0), swap_core(dy2)
    x = [jnp.concatenate([x0, x1], axis=0), jnp.concatenate([x2, x3], axis=0)]
    dy = [jnp.concatenate([dy0, dy1], axis=0), jnp.concatenate([dy2, dy3], axis=0)]

    def forward(a, w):
        mine = jnp.dot(a, w, preferred_element_type=f32).astype(bf16)
        return mine, swap_row(mine)

    gu = [[None, None], [None, None]]
    early = [forward(x0, gu_w[0]), forward(x1, gu_w[0])]
    gu[0][0] = tuple(jnp.concatenate([early[0][i], early[1][i]], axis=0) for i in range(2))
    gu[0][1] = forward(x[1], gu_w[0])
    gu[1][0] = forward(x[0], gu_w[1])
    gu[1][1] = forward(x[1], gu_w[1])

    def gates(band, half):
        mine, theirs = gu[band][half]
        both = mine.astype(f32) + theirs.astype(f32)
        w = bands[band][1]
        gate, up = both[:, :w], both[:, w:]
        return gate, up, jax.nn.sigmoid(gate)

    hidden = [[None, None], [None, None]]
    for band in range(2):
        for half in range(2):
            gate, up, sigma = gates(band, half)
            hidden[band][half] = (gate * sigma * up).astype(bf16)

    def reduce_groups(halves):
        sums = [
            (a[:rows].astype(f32) + swap_core(a[rows:]).astype(f32)).astype(bf16) for a in halves
        ]
        far = lax.psum_scatter(sums[1], "col", scatter_dimension=0, tiled=True)
        near = lax.psum_scatter(sums[0], "col", scatter_dimension=0, tiled=True)
        return (near.astype(f32) + swap_y(far).astype(f32)).astype(bf16)

    layer_out = reduce_groups(
        [
            jnp.dot(
                jnp.concatenate([hidden[0][half], hidden[1][half]], axis=1),
                down_w,
                preferred_element_type=f32,
            ).astype(bf16)
            for half in range(2)
        ]
    )

    def spread(a):
        far = swap_y(a)
        return [a, swap_core(a), far, swap_core(far)]

    pos = jnp.stack([me, me ^ 1, me ^ 2, me ^ 3]).astype(jnp.int32)
    down_wgrad, gu_wgrad = None, None
    for band in range(2):
        o, w = bands[band]
        part = contract_rows(hidden[band][0], dy[0]) + contract_rows(hidden[band][1], dy[1])
        down_wgrad = place(pos, spread(part.astype(bf16)), down_wgrad, total, o, w, 1, 0)

    grads = [[None, None], [None, None]]
    for band in range(2):
        o, w = bands[band]
        for half in (1, 0):
            mine = contract_cols(dy[half], d_w[band]).astype(bf16)
            hidden_grad = mine.astype(f32) + swap_row(mine).astype(f32)
            gate, up, sigma = gates(band, half)
            gate_grad = hidden_grad * up * sigma * (1.0 + gate * (1.0 - sigma))
            up_grad = hidden_grad * (gate * sigma)
            grads[band][half] = jnp.concatenate(
                [gate_grad.astype(bf16), up_grad.astype(bf16)], axis=1
            )
        part = contract_rows(x[0], grads[band][0]) + contract_rows(x[1], grads[band][1])
        gu_wgrad = place(pos, spread(part.astype(bf16)), gu_wgrad, total, o, w, 2, 1)

    input_grad = reduce_groups(
        [
            (
                contract_cols(grads[0][half], gu_w[0]) + contract_cols(grads[1][half], gu_w[1])
            ).astype(bf16)
            for half in range(2)
        ]
    )
    return layer_out, input_grad, gu_wgrad[0], gu_wgrad[1], down_wgrad[0]


def local(tokens, cotangent, gate_weight, up_weight, down_weight):
    f32 = jnp.float32
    whole_x, whole_dy = (
        lax.all_gather(tokens, "col", axis=1, tiled=True),
        lax.all_gather(cotangent, "col", axis=1, tiled=True),
    )
    width = gate_weight.shape[1]
    rows = whole_x
    stacked = lax.psum_scatter(
        jnp.concatenate(
            [
                jnp.dot(rows, gate_weight, preferred_element_type=f32),
                jnp.dot(rows, up_weight, preferred_element_type=f32),
            ],
            axis=1,
        ).astype(jnp.bfloat16),
        "row",
        scatter_dimension=0,
        tiled=True,
    ).astype(jnp.float32)
    gate = stacked[:, :width]
    up = stacked[:, width:]
    sigma = jax.nn.sigmoid(gate)
    silu_gate = gate * sigma
    hidden = (silu_gate * up).astype(jnp.bfloat16)
    hidden_all = lax.all_gather(hidden, "row", axis=0, tiled=True)
    out_terms = jnp.dot(hidden_all, down_weight, preferred_element_type=f32)
    layer_out = lax.psum_scatter(
        out_terms.astype(jnp.bfloat16), "col", scatter_dimension=0, tiled=True
    )
    down_part = contract_rows(hidden_all, whole_dy).astype(jnp.bfloat16)
    rows = whole_dy
    hidden_grad = lax.psum_scatter(
        contract_cols(rows, down_weight).astype(jnp.bfloat16),
        "row",
        scatter_dimension=0,
        tiled=True,
    ).astype(jnp.float32)
    gate_grad = (hidden_grad * up * sigma * (1.0 + gate * (1.0 - sigma))).astype(jnp.bfloat16)
    up_grad = (hidden_grad * silu_gate).astype(jnp.bfloat16)
    gate_all, up_all = (
        lax.all_gather(gate_grad, "row", axis=0, tiled=True),
        lax.all_gather(up_grad, "row", axis=0, tiled=True),
    )
    input_grad = lax.psum_scatter(
        (contract_cols(gate_all, gate_weight) + contract_cols(up_all, up_weight)).astype(
            jnp.bfloat16
        ),
        "col",
        scatter_dimension=0,
        tiled=True,
    )
    gate_part = contract_rows(whole_x, gate_all).astype(jnp.bfloat16)
    up_part = contract_rows(whole_x, up_all).astype(jnp.bfloat16)
    gate_sum, up_sum, down_sum = (
        lax.psum(gate_part.astype(f32).astype(jnp.bfloat16), "dp").astype(jnp.float32),
        lax.psum(up_part.astype(f32).astype(jnp.bfloat16), "dp").astype(jnp.float32),
        lax.psum(down_part.astype(f32).astype(jnp.bfloat16), "dp").astype(jnp.float32),
    )
    gate_wgrad = gate_sum.astype(jnp.bfloat16)
    up_wgrad = up_sum.astype(jnp.bfloat16)
    down_wgrad = down_sum.astype(jnp.bfloat16)
    return (layer_out, input_grad, gate_wgrad, up_wgrad, down_wgrad)


def solution(mesh):
    in_specs = (
        P("dp", ("row", "col")),
        P("dp", ("row", "col")),
        P("row", "col"),
        P("row", "col"),
        P("col", "row"),
    )
    out_specs = (
        P(("dp", "col"), "row"),
        P(("dp", "col"), "row"),
        P("row", "col"),
        P("row", "col"),
        P("col", "row"),
    )
    n_dp, n_row, n_col = (mesh.shape[name] for name in ("dp", "row", "col"))

    def run(tokens, cotangent, gate_weight, up_weight, down_weight):
        units = gate_weight.shape[1] // (n_col * n_dp)
        split = n_dp == 4 and n_row == 2 and units % LANES == 0 and units >= 3 * LANES
        return jax.shard_map(
            local_units if split else local,
            mesh=mesh,
            in_specs=in_specs,
            out_specs=out_specs,
            check_vma=False,
        )(tokens, cotangent, gate_weight, up_weight, down_weight)

    return run
```

```python
import functools

import jax
import jax.numpy as jnp
from jax import lax
from jax.experimental import pallas as pl
from jax.experimental.pallas import tpu as pltpu
from jax.sharding import PartitionSpec as P

LANES = 128


def contract_rows(left, right):
    return lax.dot_general(
        left, right, (((0,), (0,)), ((), ())), preferred_element_type=jnp.float32
    )


def contract_cols(left, right):
    return lax.dot_general(
        left, right, (((1,), (1,)), ((), ())), preferred_element_type=jnp.float32
    )


def place_body(parts, outs, aliased, pos_ref, *refs):
    ins = refs[: parts * outs]
    results = refs[parts * outs + aliased :]
    step = pl.program_id(0)
    for part in range(parts):

        @pl.when(step == part)
        def _(part=part):
            for out in range(outs):
                results[out][...] = ins[part * outs + out][...]


def place(pos, pieces, previous, total, offset, width, outs, axis):
    parts = len(pieces)
    steps = width // LANES
    other = pieces[0].shape[1 - axis]
    units = parts * total

    def at(index):
        return (index, 0) if axis == 0 else (0, index)

    block = (LANES, other) if axis == 0 else (other, LANES)

    def in_spec(part, out):
        def index(j, i, pos_ref):
            own = jnp.where(j == part, i, jnp.where(j < part, 0, steps - 1))
            return at(out * steps + own)

        return pl.BlockSpec(block, index)

    def out_index(j, i, pos_ref):
        return at(pos_ref[j] * (total // LANES) + offset // LANES + i)

    shape = (units, other) if axis == 0 else (other, units)
    operands = [pieces[part] for part in range(parts) for _ in range(outs)]
    in_specs = [in_spec(part, out) for part in range(parts) for out in range(outs)]
    aliases = {}
    if previous is not None:
        for out in range(outs):
            aliases[1 + len(operands)] = out
            operands.append(previous[out])
            in_specs.append(pl.BlockSpec(memory_space=pl.ANY))
    moved = 4 * parts * outs * width * other
    return pl.pallas_call(
        functools.partial(place_body, parts, outs, 0 if previous is None else outs),
        out_shape=[jax.ShapeDtypeStruct(shape, jnp.bfloat16)] * outs,
        grid_spec=pltpu.PrefetchScalarGridSpec(
            num_scalar_prefetch=1,
            grid=(parts, steps),
            in_specs=in_specs,
            out_specs=[pl.BlockSpec(block, out_index)] * outs,
        ),
        input_output_aliases=aliases,
        compiler_params=pltpu.CompilerParams(vmem_limit_bytes=32 * 2**20),
        cost_estimate=pl.CostEstimate(flops=0, bytes_accessed=moved, transcendentals=0),
    )(pos, *operands)


def local_units(tokens, cotangent, gate_weight, up_weight, down_weight):
    f32, bf16 = jnp.float32, jnp.bfloat16
    me = lax.axis_index("dp")
    total = gate_weight.shape[1] // 4
    first = -(-total // 512) * 256
    bands = ((0, first), (first, total - first))
    rows = tokens.shape[0]

    def swap_row(a):
        return lax.ppermute(a, "row", [(0, 1), (1, 0)])

    def swap_core(a):
        return lax.ppermute(a, "dp", [(i, i ^ 1) for i in range(4)])

    def swap_y(a):
        return lax.ppermute(a, "dp", [(i, i ^ 2) for i in range(4)])

    start = me * total
    gate_w = lax.dynamic_slice_in_dim(gate_weight, start, total, 1)
    up_w = lax.dynamic_slice_in_dim(up_weight, start, total, 1)
    down_w = lax.dynamic_slice_in_dim(down_weight, start, total, 0)
    gu_w = [jnp.concatenate([gate_w[:, o : o + w], up_w[:, o : o + w]], axis=1) for o, w in bands]
    d_w = [down_w[o : o + w] for o, w in bands]

    def after(done, *values):
        tied = lax.optimization_barrier((values, done))[0]
        return tied if len(values) > 1 else tied[0]

    def halves(near, far):
        return jnp.concatenate([near, far], axis=0)

    def forward(a, w):
        return jnp.dot(a, w, preferred_element_type=f32).astype(bf16)

    def gates(band, mine, theirs):
        both = mine.astype(f32) + theirs.astype(f32)
        w = bands[band][1]
        gate, up = both[:, :w], both[:, w:]
        return gate, up, jax.nn.sigmoid(gate)

    def activate(band, gu):
        gate, up, sigma = gates(band, *gu)
        return (gate * sigma * up).astype(bf16)

    def backward(band, gu, mine, theirs):
        gate, up, sigma = gates(band, *gu)
        hidden_grad = mine.astype(f32) + theirs.astype(f32)
        gate_grad = hidden_grad * up * sigma * (1.0 + gate * (1.0 - sigma))
        up_grad = hidden_grad * (gate * sigma)
        return jnp.concatenate([gate_grad.astype(bf16), up_grad.astype(bf16)], axis=1)

    def core_sum(a):
        return (a[:rows].astype(f32) + swap_core(a[rows:]).astype(f32)).astype(bf16)

    def scatter(a):
        return lax.psum_scatter(a, "col", scatter_dimension=0, tiled=True)

    def spread(a, far):
        return [a, swap_core(a), far, swap_core(far)]

    pos = jnp.stack([me, me ^ 1, me ^ 2, me ^ 3]).astype(jnp.int32)

    x0 = lax.all_gather(tokens, "col", axis=1, tiled=True)
    dy0 = lax.all_gather(after(x0, cotangent), "col", axis=1, tiled=True)
    x2 = swap_y(x0)
    x1 = swap_core(x0)

    a0 = forward(x0, gu_w[0])
    a0_in = swap_row(a0)
    a1 = forward(after(a0, x1), gu_w[0])
    a1_in = swap_row(a1)
    x_near = halves(x0, x1)
    b_near = forward(after(a1, x_near), gu_w[1])
    b_near_in = swap_row(b_near)
    ha0 = activate(0, after(b_near, a0, a0_in))
    dy0 = after(ha0, dy0)
    dy2 = swap_y(dy0)
    dy1 = swap_core(dy0)

    x3 = swap_core(x2)
    x_far = halves(x2, x3)
    a_far = forward(after(ha0, x_far), gu_w[0])
    a_far_in = swap_row(a_far)
    ha1 = activate(0, after(a_far, a1, a1_in))
    b_far = forward(after(ha1, x_far), gu_w[1])
    b_far_in = swap_row(b_far)
    dy_near = halves(dy0, dy1)
    ga_near = contract_cols(after(b_far, dy_near), d_w[0]).astype(bf16)
    ga_near_in = swap_row(ga_near)
    hb_near = activate(1, after(ga_near, b_near, b_near_in))
    ha_near = halves(ha0, ha1)
    h_near = jnp.concatenate([ha_near, hb_near], axis=1)
    out_near = forward(h_near, down_w)
    dy3 = swap_core(dy2)
    dy_far = halves(dy2, dy3)
    ga_far = contract_cols(after(out_near, dy_far), d_w[0]).astype(bf16)
    ga_far_in = swap_row(ga_far)
    near_sum = core_sum(after(ga_far, out_near))
    near = scatter(near_sum)

    ha_far = activate(0, after(ga_far, a_far, a_far_in))
    down_a = (contract_rows(ha_near, dy_near) + contract_rows(ha_far, dy_far)).astype(bf16)
    down_a_in = swap_y(down_a)
    gb_far = contract_cols(after((down_a, near_sum), dy_far), d_w[1]).astype(bf16)
    gb_far_in = swap_row(gb_far)
    gb_near = contract_cols(after(gb_far, dy_near), d_w[1]).astype(bf16)
    gb_near_in = swap_row(gb_near)
    hb_far = activate(1, after(gb_near, b_far, b_far_in))
    h_tied = after((hb_far, ga_near_in, near), hb_near, hb_far)
    down_b = (contract_rows(h_tied[0], dy_near) + contract_rows(h_tied[1], dy_far)).astype(bf16)
    out_far = forward(
        after((down_b, down_a_in, ga_far_in), jnp.concatenate([ha_far, hb_far], axis=1)), down_w
    )
    far_sum = core_sum(out_far)
    far = scatter(far_sum)
    down_b_in = swap_y(down_b)
    down_wgrad = place(
        pos, list(after(out_far, *spread(down_a, down_a_in))), None, total, *bands[0], 1, 0
    )

    ga_tied = after((far_sum, down_wgrad, ga_far_in), a0, a0_in, a1, a1_in, ga_near, ga_near_in)
    qa_near = backward(
        0, (halves(ga_tied[0], ga_tied[2]), halves(ga_tied[1], ga_tied[3])), *ga_tied[4:]
    )
    ga_tied = after((qa_near, down_b_in), a_far, a_far_in, ga_far, ga_far_in)
    qa_far = backward(0, ga_tied[:2], *ga_tied[2:])

    def weight_part(near, far):
        return (contract_rows(x_near, near) + contract_rows(x_far, far)).astype(bf16)

    wa, wb = bands[0][1], bands[1][1]
    gate_a = weight_part(qa_near[:, :wa], qa_far[:, :wa])
    gate_a_in = swap_y(gate_a)
    gb_tied = after((gate_a, gb_near_in), b_far, b_far_in, gb_far, gb_far_in)
    qb_far = backward(1, gb_tied[:2], *gb_tied[2:])
    ig_far = (contract_cols(qa_far, gu_w[0]) + contract_cols(qb_far, gu_w[1])).astype(bf16)
    ig_far_sum = core_sum(ig_far)
    ig_far_out = scatter(ig_far_sum)
    q_tied = after((ig_far, gb_near_in, gate_a_in, far), qa_near, qa_far)
    up_a = weight_part(q_tied[0][:, wa:], q_tied[1][:, wa:])
    up_a_in = swap_y(up_a)
    gb_tied = after((up_a, ig_far_sum), b_near, b_near_in, gb_near, gb_near_in)
    qb_near = backward(1, gb_tied[:2], *gb_tied[2:])
    q_tied = (qa_near, qb_near)
    ig_near = (contract_cols(q_tied[0], gu_w[0]) + contract_cols(q_tied[1], gu_w[1])).astype(bf16)
    ig_near_sum = core_sum(ig_near)
    ig_near_out = scatter(ig_near_sum)
    q_tied = after(ig_near, qb_near, qb_far)
    gate_b = weight_part(q_tied[0][:, :wb], q_tied[1][:, :wb])
    gate_b_in = swap_y(gate_b)
    q_tied = after((gate_b, ig_near_sum), qb_near, qb_far)
    up_b = weight_part(q_tied[0][:, wb:], q_tied[1][:, wb:])
    up_b_in = swap_y(up_b)

    down_pieces = list(after(up_b, *spread(down_b, down_b_in)))
    down_wgrad = place(pos, down_pieces, down_wgrad, total, *bands[1], 1, 0)
    gate_pieces = list(after(down_wgrad, *spread(gate_a, gate_a_in)))
    gate_wgrad = place(pos, gate_pieces, None, total, *bands[0], 1, 1)
    layer_out = (near.astype(f32) + swap_y(after(gate_wgrad, far)).astype(f32)).astype(bf16)
    up_pieces = list(after((gate_wgrad, ig_far_out), *spread(up_a, up_a_in)))
    up_wgrad = place(pos, up_pieces, None, total, *bands[0], 1, 1)
    gate_pieces = list(after(up_wgrad, *spread(gate_b, gate_b_in)))
    gate_wgrad = place(pos, gate_pieces, gate_wgrad, total, *bands[1], 1, 1)
    up_wgrad = place(pos, spread(up_b, up_b_in), up_wgrad, total, *bands[1], 1, 1)
    input_grad = (ig_near_out.astype(f32) + swap_y(ig_far_out).astype(f32)).astype(bf16)
    return layer_out, input_grad, gate_wgrad[0], up_wgrad[0], down_wgrad[0]


def local(tokens, cotangent, gate_weight, up_weight, down_weight):
    f32 = jnp.float32
    whole_x, whole_dy = (
        lax.all_gather(tokens, "col", axis=1, tiled=True),
        lax.all_gather(cotangent, "col", axis=1, tiled=True),
    )
    width = gate_weight.shape[1]
    rows = whole_x
    stacked = lax.psum_scatter(
        jnp.concatenate(
            [
                jnp.dot(rows, gate_weight, preferred_element_type=f32),
                jnp.dot(rows, up_weight, preferred_element_type=f32),
            ],
            axis=1,
        ).astype(jnp.bfloat16),
        "row",
        scatter_dimension=0,
        tiled=True,
    ).astype(jnp.float32)
    gate = stacked[:, :width]
    up = stacked[:, width:]
    sigma = jax.nn.sigmoid(gate)
    silu_gate = gate * sigma
    hidden = (silu_gate * up).astype(jnp.bfloat16)
    hidden_all = lax.all_gather(hidden, "row", axis=0, tiled=True)
    out_terms = jnp.dot(hidden_all, down_weight, preferred_element_type=f32)
    layer_out = lax.psum_scatter(
        out_terms.astype(jnp.bfloat16), "col", scatter_dimension=0, tiled=True
    )
    down_part = contract_rows(hidden_all, whole_dy).astype(jnp.bfloat16)
    rows = whole_dy
    hidden_grad = lax.psum_scatter(
        contract_cols(rows, down_weight).astype(jnp.bfloat16),
        "row",
        scatter_dimension=0,
        tiled=True,
    ).astype(jnp.float32)
    gate_grad = (hidden_grad * up * sigma * (1.0 + gate * (1.0 - sigma))).astype(jnp.bfloat16)
    up_grad = (hidden_grad * silu_gate).astype(jnp.bfloat16)
    gate_all, up_all = (
        lax.all_gather(gate_grad, "row", axis=0, tiled=True),
        lax.all_gather(up_grad, "row", axis=0, tiled=True),
    )
    input_grad = lax.psum_scatter(
        (contract_cols(gate_all, gate_weight) + contract_cols(up_all, up_weight)).astype(
            jnp.bfloat16
        ),
        "col",
        scatter_dimension=0,
        tiled=True,
    )
    gate_part = contract_rows(whole_x, gate_all).astype(jnp.bfloat16)
    up_part = contract_rows(whole_x, up_all).astype(jnp.bfloat16)
    gate_sum, up_sum, down_sum = (
        lax.psum(gate_part.astype(f32).astype(jnp.bfloat16), "dp").astype(jnp.float32),
        lax.psum(up_part.astype(f32).astype(jnp.bfloat16), "dp").astype(jnp.float32),
        lax.psum(down_part.astype(f32).astype(jnp.bfloat16), "dp").astype(jnp.float32),
    )
    gate_wgrad = gate_sum.astype(jnp.bfloat16)
    up_wgrad = up_sum.astype(jnp.bfloat16)
    down_wgrad = down_sum.astype(jnp.bfloat16)
    return (layer_out, input_grad, gate_wgrad, up_wgrad, down_wgrad)


def solution(mesh):
    in_specs = (
        P("dp", ("row", "col")),
        P("dp", ("row", "col")),
        P("row", "col"),
        P("row", "col"),
        P("col", "row"),
    )
    out_specs = (
        P(("dp", "col"), "row"),
        P(("dp", "col"), "row"),
        P("row", "col"),
        P("row", "col"),
        P("col", "row"),
    )
    n_dp, n_row, n_col = (mesh.shape[name] for name in ("dp", "row", "col"))

    def run(tokens, cotangent, gate_weight, up_weight, down_weight):
        units = gate_weight.shape[1] // (n_col * n_dp)
        split = n_dp == 4 and n_row == 2 and units % LANES == 0 and units >= 3 * LANES
        return jax.shard_map(
            local_units if split else local,
            mesh=mesh,
            in_specs=in_specs,
            out_specs=out_specs,
            check_vma=False,
        )(tokens, cotangent, gate_weight, up_weight, down_weight)

    return run
```
